32 devices in a mesh: grp: 2 (over y), row: 4 (over z), col: 4 (over x, core).
Axes of the slice: x: 2, y: 2, z: 4, core: 2. Of those that a mesh axis runs over, the one named last changes fastest.
Arguments:
- pair: bfloat16 [128, 64, 128], P(('grp', 'row'), 'col'), parts along dimension 0, may hold values from -6 to 6
- cotangent: bfloat16 [128, 64, 128], P(('grp', 'row'), 'col'), parts along dimension 0, may hold values from -6 to 6
- weight_codes: int32 [6, 128, 128], replicated, may hold values from -127 to 127
- exponents: int32 [6, 4], replicated, may hold values from -11 to -9
- residue_mask: int32 [128], P('grp'), parts along dimension 0, may hold values 0 or 1
Outputs:
- pair_grad: float32 [128, 64, 128], P(('grp', 'row'), 'col'), parts along dimension 0
The draws below stay inside these ranges and needn't reach their ends.
There are 2 independent parts, one for each index of `grp`. The reference program is written for one: setup_inputs(seed, part) draws one part's arguments, and reference() takes and returns one part's arrays. A program takes and returns all parts, laid end to end along the dimension named above; an argument that names none is the same for every part. Nothing has to cross between parts.
All inputs are finite; a program needn't handle non-finite values.
Results may differ from the reference program's by a relative error of at most 0.012.
Values may be sent and summed in bfloat16 or wider, within the bound.
A program may use at most 64 MiB of HBM per device.

```python
import jax
import jax.numpy as jnp
from jax import lax

CZ = 128
QBLOCK = 32
N = 64


def set_ends(drawn, own_key, least, top_value):
    dims = drawn.shape
    index_at = [jax.random.randint(jax.random.fold_in(own_key, axis), (), 0, dims[axis]) for axis in range(len(dims))]
    drawn = drawn.at[tuple(index_at)].set(least)
    longest = dims.index(max(dims))
    index_at[longest] = (index_at[longest] + 1) % dims[longest]
    return drawn.at[tuple(index_at)].set(top_value)


def block_scale(rng, extent, shards, low, largest):
    def one(dim, blocks):
        heights = jax.random.uniform(jax.random.fold_in(jax.random.fold_in(rng, 6), dim), (blocks,), jnp.float32, low / len(shards), largest / len(shards))
        return jnp.repeat(jnp.exp(heights), extent[dim] // blocks).reshape((-1,) + (1,) * (len(extent) - dim - 1))

    level = one(*shards[0])
    for cut in shards[1:]:
        level = level * one(*cut)
    return level


def gaussian(key, dims, scale, reach, cuts=(), dtype=jnp.bfloat16):
    array = jax.random.normal(key, dims, jnp.float32) * scale
    if len(cuts) > 0:
        array = block_scale(key, dims, cuts, -0.22, 0.18) * array
    return jnp.clip(array, min=-reach, max=reach).astype(dtype)


def setup_inputs(seed: int = 0, part: int = 0) -> dict:
    splits = jax.random.split(jax.random.key(seed), 6)
    part_keys = jax.random.split(jax.random.fold_in(splits[5], part), 6)
    pair = gaussian(part_keys[0], (N, N, CZ), 1.0, 6.0, ((0, 4), (1, 4)))
    cotangent = gaussian(part_keys[1], (N, N, CZ), 1.0, 6.0, ((0, 4), (1, 4)))
    weight_codes = set_ends(jax.random.randint(splits[2], (6, CZ, CZ), -127, 128), jax.random.fold_in(splits[2], 1), -127, 127).astype(jnp.int32)
    exponents = set_ends(jax.random.randint(splits[3], (6, CZ // QBLOCK), -11, -8), jax.random.fold_in(splits[3], 1), -11, (-8) - 1).astype(jnp.int32)
    residue_mask = set_ends((jax.random.randint(part_keys[4], (N,), 0, 8) < 7).astype(jnp.int32), jax.random.fold_in(part_keys[4], 1), 0, 1)
    return {"pair": pair, "cotangent": cotangent, "weight_codes": weight_codes, "exponents": exponents, "residue_mask": residue_mask}


def layer_norm(values):
    average = lax.optimization_barrier(jnp.mean(values, axis=-1, keepdims=True))
    centered = values - average
    inverse = lax.rsqrt(lax.optimization_barrier(jnp.mean(centered * centered, axis=-1, keepdims=True)) + 1e-05)
    return (centered * inverse, inverse)

def norm_back(normed, inverse, upstream):
    first = lax.optimization_barrier(jnp.mean(upstream, axis=-1, keepdims=True))
    second = lax.optimization_barrier(jnp.mean(upstream * normed, axis=-1, keepdims=True))
    return inverse * (upstream - first - normed * second)

def restore_weights(weight_codes, exponents):
    matrices = weight_codes.shape[0]
    width = weight_codes.shape[1]
    blocks = exponents.shape[1]
    factor = jnp.exp2(exponents.astype(jnp.float32))[:, :, None, None]
    scaled = weight_codes.astype(jnp.float32).reshape(matrices, blocks, width // blocks, width) * factor
    return scaled.reshape(matrices, width, width).astype(jnp.bfloat16)

def reference(pair, cotangent, weight_codes, exponents, residue_mask):
    weights = restore_weights(weight_codes, exponents)
    stacked = jnp.concatenate([weights[0], weights[1], weights[2], weights[3], weights[4]], axis=1)
    normed, inverse = layer_norm(pair.astype(jnp.float32))
    pair_normed = normed.astype(jnp.bfloat16)
    projected = jnp.dot(pair_normed.reshape(N * N, CZ), stacked, preferred_element_type=jnp.float32).reshape(N, N, 5 * CZ)
    left_gate = projected[:, :, 0:CZ]
    left_value = projected[:, :, CZ:2 * CZ]
    right_gate = projected[:, :, 2 * CZ:3 * CZ]
    right_value = projected[:, :, 3 * CZ:4 * CZ]
    out_gate = projected[:, :, 4 * CZ:5 * CZ]
    keep = residue_mask.astype(jnp.float32)
    pair_mask = (keep[:, None] * keep[None, :])[:, :, None]
    left_sigmoid = jax.nn.sigmoid(left_gate)
    right_sigmoid = jax.nn.sigmoid(right_gate)
    left = (pair_mask * left_sigmoid * left_value).astype(jnp.bfloat16)
    right = (pair_mask * right_sigmoid * right_value).astype(jnp.bfloat16)
    update = jnp.einsum('ikc,jkc->ijc', left.astype(jnp.float32), right.astype(jnp.float32))
    update_normed, update_inverse = layer_norm(update)
    out_value = jnp.dot(update_normed.astype(jnp.bfloat16).reshape(N * N, CZ), weights[5], preferred_element_type=jnp.float32).reshape(N, N, CZ)
    gate = jax.nn.sigmoid(out_gate)
    upstream = cotangent.astype(jnp.float32)
    grad_value = (upstream * gate).astype(jnp.bfloat16)
    grad_gate = (upstream * out_value * gate * (1.0 - gate)).astype(jnp.bfloat16)
    grad_normed = jnp.dot(grad_value.reshape(N * N, CZ), weights[5].T, preferred_element_type=jnp.float32).reshape(N, N, CZ)
    update_grad = norm_back(update_normed, update_inverse, grad_normed).astype(jnp.bfloat16)
    left_grad = jnp.einsum('ijc,jkc->ikc', update_grad.astype(jnp.float32), right.astype(jnp.float32))
    right_grad = jnp.einsum('ijc,ikc->jkc', update_grad.astype(jnp.float32), left.astype(jnp.float32))
    left_gate_grad = (left_grad * pair_mask * left_value * left_sigmoid * (1.0 - left_sigmoid)).astype(jnp.bfloat16)
    left_value_grad = (left_grad * pair_mask * left_sigmoid).astype(jnp.bfloat16)
    right_gate_grad = (right_grad * pair_mask * right_value * right_sigmoid * (1.0 - right_sigmoid)).astype(jnp.bfloat16)
    right_value_grad = (right_grad * pair_mask * right_sigmoid).astype(jnp.bfloat16)
    joined = jnp.concatenate([left_gate_grad, left_value_grad, right_gate_grad, right_value_grad, grad_gate], axis=-1)
    normed_grad = jnp.dot(joined.reshape(N * N, 5 * CZ), stacked.T, preferred_element_type=jnp.float32).reshape(N, N, CZ)
    return norm_back(normed, inverse, normed_grad)
```

```python
import functools

import jax
import jax.numpy as jnp
from jax import lax
from jax.experimental import pallas as pl
from jax.experimental.pallas import tpu as pltpu
from jax.sharding import PartitionSpec as P

F32 = jnp.float32
BF16 = jnp.bfloat16
MESH = pl.DeviceIdType.MESH
GROUP = 4


def partner(me, d, n):
    if n & (n - 1):
        return lax.rem(me + d, n)
    out = me
    bit = 1
    while bit < n:
        if d & bit:
            out = out + bit - 2 * bit * lax.rem(lax.div(me, bit), 2)
        bit *= 2
    return out


def dot(a, b):
    return jnp.dot(a, b, preferred_element_type=F32)


def dot_t(a, b):
    return lax.dot_general(a, b, (((1,), (1,)), ((), ())), preferred_element_type=F32)


def contract(side, rows_ref, row_base, outer, inner, mat_ref, mat_base, emit):
    def body(g, carry):
        first = g * GROUP
        sums = [None] * GROUP
        start = row_base + first * outer
        for s in range(side):
            block = mat_ref[pl.ds(mat_base + s * side, side), :]
            for q in range(GROUP):
                row = rows_ref[pl.ds(start + q * outer + s * inner, 1), :]
                term = row * block
                sums[q] = term if sums[q] is None else sums[q] + term
        for q in range(GROUP):
            emit(pl.multiple_of((first + q) * side, side), sums[q])
        return carry

    lax.fori_loop(0, side // GROUP, body, 0)


def kernel(side, n, pair_ref, cot_ref, codes_ref, exps_ref, mask_ref, out_ref,
           w_ref, perm_ref, rbuf, rf, ubuf, sbuf, cbuf, ugf, ebuf, gbuf,
           left_f, left_t, coef, keep, lg_ref, send_sem, recv_sem):
    rows = side * side
    width = pair_ref.shape[1]
    my_row = lax.axis_index("row")
    my_col = lax.axis_index("col")
    shift = side.bit_length() - 1

    barrier = pltpu.get_barrier_semaphore()
    for d in range(1, n):
        pl.semaphore_signal(barrier, inc=1, device_id={"row": partner(my_row, d, n)}, device_id_type=MESH)
        pl.semaphore_signal(barrier, inc=1, device_id={"col": partner(my_col, d, n)}, device_id_type=MESH)

    def remote(stage, src, dst, send_slot, recv_slot, target):
        return pltpu.make_async_remote_copy(
            src_ref=src, dst_ref=dst,
            send_sem=send_sem.at[stage, send_slot], recv_sem=recv_sem.at[stage, recv_slot],
            device_id=target, device_id_type=MESH,
        )

    def wait_arrival(stage, buf, slot, axis):
        remote(stage, buf.at[slot], buf.at[slot], 0, slot, {axis: slot}).wait_recv()

    factor = jnp.exp2(exps_ref[...].astype(F32))
    blocks = exps_ref.shape[1]
    depth = width // blocks

    def restore(m):
        for b in range(blocks):
            scaled = codes_ref[m, b * depth:(b + 1) * depth, :].astype(F32) * factor[m:m + 1, b:b + 1]
            w_ref[b * depth:(b + 1) * depth, m * width:(m + 1) * width] = scaled.astype(BF16)

    def weight(first, last):
        return w_ref[:, first * width:last * width]

    for m in (2, 3):
        restore(m)

    total = mask_ref.shape[1]
    at_row = lax.broadcasted_iota(jnp.int32, (rows, total), 0)
    at_lane = lax.broadcasted_iota(jnp.int32, (rows, total), 1)
    picks = jnp.where(at_lane == my_row * side + (at_row >> shift), 1.0, 0.0) + jnp.where(
        at_lane == my_col * side + (at_row & (side - 1)), 1.0, 0.0)
    kept = jnp.broadcast_to(mask_ref[...].astype(F32), (width, total)).astype(BF16)
    pair_mask = jnp.where(dot_t(picks.astype(BF16), kept) > 1.5, 1.0, 0.0)

    x = pair_ref[...].astype(F32)
    centered = x - jnp.mean(x, axis=-1, keepdims=True)
    pair_inverse = lax.rsqrt(jnp.mean(centered * centered, axis=-1, keepdims=True) + 1e-05)
    normed = centered * pair_inverse
    pair_normed = normed.astype(BF16)

    projected = dot(pair_normed, weight(2, 4))
    gate_r, value_r = projected[:, :width], projected[:, width:]
    sig_r = jax.nn.sigmoid(gate_r)
    masked_r = pair_mask * sig_r
    right = (masked_r * value_r).astype(BF16)
    rbuf[my_row] = right
    pl.semaphore_wait(barrier, 2 * (n - 1))
    for d in range(1, n):
        remote(0, rbuf.at[my_row], rbuf.at[my_row], d, my_row, {"row": partner(my_row, d, n)}).start()
    coef[2] = masked_r * value_r * (1.0 - sig_r)
    coef[3] = masked_r
    rf[pl.ds(pl.multiple_of(my_row * rows, rows), rows), :] = right.astype(F32)

    a = lax.broadcasted_iota(jnp.int32, (rows, rows), 0)
    b = lax.broadcasted_iota(jnp.int32, (rows, rows), 1)
    perm_ref[...] = jnp.where(b == ((a & (side - 1)) << shift) + (a >> shift), 1.0, 0.0).astype(BF16)
    for m in (0, 1, 4, 5):
        restore(m)
    projected = dot(pair_normed, weight(0, 2))
    gate_l, value_l = projected[:, :width], projected[:, width:]
    sig_l = jax.nn.sigmoid(gate_l)
    masked_l = pair_mask * sig_l
    left = (masked_l * value_l).astype(BF16)
    left_f[...] = left.astype(F32)
    left_t[...] = dot(perm_ref[...], left)
    coef[0] = masked_l * value_l * (1.0 - sig_l)
    coef[1] = masked_l

    gate = jax.nn.sigmoid(dot(pair_normed, weight(4, 5)))
    upstream = cot_ref[...].astype(F32)
    gated = upstream * gate
    keep[0] = gated * (1.0 - gate)
    grad_normed = dot_t(gated.astype(BF16), weight(5, 6))
    keep[1] = grad_normed - jnp.mean(grad_normed, axis=-1, keepdims=True)

    for d in range(n):
        r = partner(my_row, d, n)
        base = pl.multiple_of(r * rows, rows)
        if d > 0:
            wait_arrival(0, rbuf, r, "row")
            rf[pl.ds(base, rows), :] = rbuf[r].astype(F32)

        def emit(o, value, d=d):
            sbuf[d, pl.ds(o, side), :] = value.astype(BF16)

        contract(side, rf, base, side, 1, left_t, 0, emit)

        @pl.when(r != my_col)
        def _():
            remote(1, sbuf.at[d], ubuf.at[my_col], d, my_col, {"col": r}).start()

        @pl.when(r == my_col)
        def _():
            ubuf[my_col] = sbuf[d]

    for d in range(1, n):
        wait_arrival(1, ubuf, partner(my_col, d, n), "col")
    update = dot(perm_ref[...], ubuf[0])
    for s in range(1, n):
        update = update + dot(perm_ref[...], ubuf[s])

    centered = update - jnp.mean(update, axis=-1, keepdims=True)
    inverse = lax.rsqrt(jnp.mean(centered * centered, axis=-1, keepdims=True) + 1e-05)
    update_normed = centered * inverse
    grad_normed = keep[1]
    second = jnp.mean(grad_normed * update_normed, axis=-1, keepdims=True)
    update_grad = (inverse * (grad_normed - update_normed * second)).astype(BF16)
    cbuf[my_col] = update_grad
    for d in range(1, n):
        remote(2, cbuf.at[my_col], cbuf.at[my_col], d, my_col, {"col": partner(my_col, d, n)}).start()
    grad_gate = (keep[0] * dot(update_normed.astype(BF16), weight(5, 6))).astype(BF16)

    for d in range(n):
        c = partner(my_col, d, n)
        base = pl.multiple_of(c * rows, rows)
        if d > 0:
            wait_arrival(2, cbuf, c, "col")
        ugf[pl.ds(base, rows), :] = cbuf[c].astype(F32)

        def emit(o, value, d=d):
            ebuf[d, pl.ds(o, side), :] = value.astype(BF16)

        contract(side, ugf, base, 1, side, left_f, 0, emit)

        @pl.when(c != my_row)
        def _():
            remote(3, ebuf.at[d], gbuf.at[my_row], d, my_row, {"row": c}).start()

        @pl.when(c == my_row)
        def _():
            gbuf[my_row] = ebuf[d]

    for d in range(n):
        c = partner(my_col, d, n)
        base = pl.multiple_of(c * rows, rows)

        def emit(o, value, d=d):
            spot = (pl.ds(o, side), slice(None))
            lg_ref[spot] = value if d == 0 else lg_ref[spot] + value

        contract(side, ugf, base, side, 1, rf, base, emit)

    left_grad = lg_ref[...]
    normed_grad = (
        dot_t((left_grad * coef[0]).astype(BF16), weight(0, 1))
        + dot_t((left_grad * coef[1]).astype(BF16), weight(1, 2))
        + dot_t(grad_gate, weight(4, 5))
    )

    for d in range(1, n):
        wait_arrival(3, gbuf, partner(my_row, d, n), "row")
    right_grad = gbuf[0].astype(F32)
    for s in range(1, n):
        right_grad = right_grad + gbuf[s].astype(F32)
    normed_grad = (
        normed_grad
        + dot_t((right_grad * coef[2]).astype(BF16), weight(2, 3))
        + dot_t((right_grad * coef[3]).astype(BF16), weight(3, 4))
    )
    first = jnp.mean(normed_grad, axis=-1, keepdims=True)
    second = jnp.mean(normed_grad * normed, axis=-1, keepdims=True)
    out_ref[...] = pair_inverse * (normed_grad - first - normed * second)

    for d in range(1, n):
        remote(0, rbuf.at[my_row], rbuf.at[my_row], d, my_row, {"row": partner(my_row, d, n)}).wait_send()
        remote(2, cbuf.at[my_col], cbuf.at[my_col], d, my_col, {"col": partner(my_col, d, n)}).wait_send()
    for d in range(n):
        r = partner(my_row, d, n)
        c = partner(my_col, d, n)

        @pl.when(r != my_col)
        def _():
            remote(1, sbuf.at[d], ubuf.at[my_col], d, my_col, {"col": r}).wait_send()

        @pl.when(c != my_row)
        def _():
            remote(3, ebuf.at[d], gbuf.at[my_row], d, my_row, {"row": c}).wait_send()


def per_device(n, pair, cotangent, weight_codes, exponents, residue_mask):
    side = pair.shape[0]
    width = pair.shape[2]
    rows = side * side
    matrices = weight_codes.shape[0]
    slots = (n, rows, width)
    vmem = pl.BlockSpec(memory_space=pltpu.VMEM)
    out = pl.pallas_call(
        functools.partial(kernel, side, n),
        out_shape=jax.ShapeDtypeStruct((rows, width), F32),
        in_specs=[vmem] * 5,
        out_specs=vmem,
        scratch_shapes=[
            pltpu.VMEM((width, matrices * width), BF16),
            pltpu.VMEM((rows, rows), BF16),
            pltpu.VMEM(slots, BF16),
            pltpu.VMEM((n * rows, width), F32),
            pltpu.VMEM(slots, BF16),
            pltpu.VMEM(slots, BF16),
            pltpu.VMEM(slots, BF16),
            pltpu.VMEM((n * rows, width), F32),
            pltpu.VMEM(slots, BF16),
            pltpu.VMEM(slots, BF16),
            pltpu.VMEM((rows, width), F32),
            pltpu.VMEM((rows, width), F32),
            pltpu.VMEM((4, rows, width), F32),
            pltpu.VMEM((2, rows, width), F32),
            pltpu.VMEM((rows, width), F32),
            pltpu.SemaphoreType.DMA((4, n)),
            pltpu.SemaphoreType.DMA((4, n)),
        ],
        compiler_params=pltpu.CompilerParams(
            collective_id=0, has_side_effects=True, vmem_limit_bytes=40 * 1024 * 1024
        ),
    )(
        pair.reshape(rows, width),
        cotangent.reshape(rows, width),
        weight_codes,
        exponents,
        residue_mask.reshape(1, -1),
    )
    return out.reshape(pair.shape)


def solution(mesh):
    in_specs = (P(("grp", "row"), "col", None), P(("grp", "row"), "col", None), P(), P(), P("grp"))
    out_specs = P(("grp", "row"), "col", None)
    n = mesh.shape["row"]
    assert n == mesh.shape["col"]
    return jax.shard_map(
        functools.partial(per_device, n), mesh=mesh, in_specs=in_specs, out_specs=out_specs, check_vma=False
    )
```

```python
import functools

import jax
import jax.numpy as jnp
from jax import lax
from jax.experimental import pallas as pl
from jax.experimental.pallas import tpu as pltpu
from jax.sharding import PartitionSpec as P

F32 = jnp.float32
BF16 = jnp.bfloat16
MESH = pl.DeviceIdType.MESH
GROUP = 4
VMEM_LIMIT = 63 * 1024 * 1024


def partner(me, d, n):
    if n & (n - 1):
        return lax.rem(me + d, n)
    out = me
    bit = 1
    while bit < n:
        if d & bit:
            out = out + bit - 2 * bit * lax.rem(lax.div(me, bit), 2)
        bit *= 2
    return out


def dot(a, b):
    return jnp.dot(a, b, preferred_element_type=F32)


def dot_t(a, b):
    return lax.dot_general(a, b, (((1,), (1,)), ((), ())), preferred_element_type=F32)


def contract(side, rows_ref, row_base, outer, inner, mat_ref, mat_base, emit):
    def body(g, carry):
        first = g * GROUP
        sums = [None] * GROUP
        start = row_base + first * outer
        for s in range(side):
            block = mat_ref[pl.ds(mat_base + s * side, side), :]
            for q in range(GROUP):
                row = rows_ref[pl.ds(start + q * outer + s * inner, 1), :]
                term = row * block
                sums[q] = term if sums[q] is None else sums[q] + term
        for q in range(GROUP):
            emit(pl.multiple_of((first + q) * side, side), sums[q])
        return carry

    lax.fori_loop(0, side // GROUP, body, 0)


def kernel(side, n, pair_hbm, cot_hbm, codes_hbm, exps_hbm, mask_hbm, out_ref,
           pair_ref, cot_ref, codes_ref, exps_ref, mask_ref, load_sem, w_ref, perm_ref,
           own, rbuf, rf, lbuf, left_f, left_t, upd, cbuf, ugf, ebuf, gbuf, pbuf, hbuf,
           coef, keep, lg_ref, send_sem, recv_sem):
    rows = side * side
    width = pair_ref.shape[1]
    matrices = codes_ref.shape[0]
    loads = [
        pltpu.make_async_copy(src, dst, load_sem.at[i])
        for i, (src, dst) in enumerate([
            (pair_hbm, pair_ref),
            (codes_hbm.at[pl.ds(2, 2)], codes_ref.at[pl.ds(2, 2)]),
            (exps_hbm, exps_ref),
            (mask_hbm, mask_ref),
            (codes_hbm.at[pl.ds(0, 2)], codes_ref.at[pl.ds(0, 2)]),
            (codes_hbm.at[pl.ds(4, matrices - 4)], codes_ref.at[pl.ds(4, matrices - 4)]),
            (cot_hbm, cot_ref),
        ])
    ]
    for load in loads:
        load.start()
    my_row = lax.axis_index("row")
    my_col = lax.axis_index("col")
    shift = side.bit_length() - 1

    diagonal = my_row == my_col
    elsewhere = jnp.logical_not(diagonal)
    barrier = pltpu.get_barrier_semaphore()

    def greet(target):
        pl.semaphore_signal(barrier, inc=1, device_id=target, device_id_type=MESH)

    for d in range(1, n):
        greet({"row": partner(my_row, d, n)})
        greet({"col": partner(my_col, d, n)})
        greet({"row": my_col, "col": partner(my_col, d, n)})

    @pl.when(elsewhere)
    def _():
        greet({"row": my_col, "col": my_col})

    def remote(stage, src, dst, send_slot, recv_slot, target):
        return pltpu.make_async_remote_copy(
            src_ref=src, dst_ref=dst,
            send_sem=send_sem.at[stage, send_slot], recv_sem=recv_sem.at[stage, recv_slot],
            device_id=target, device_id_type=MESH,
        )

    def wait_arrival(stage, buf, slot, axis):
        remote(stage, buf.at[slot], buf.at[slot], 0, slot, {axis: slot}).wait_recv()

    for load in loads[:4]:
        load.wait()

    factor = jnp.exp2(exps_ref[...].astype(F32))
    blocks = exps_ref.shape[0]
    depth = width // blocks

    def restore(m):
        for b in range(blocks):
            scaled = codes_ref[m, b * depth:(b + 1) * depth, :].astype(F32) * factor[b:b + 1, m:m + 1]
            w_ref[b * depth:(b + 1) * depth, m * width:(m + 1) * width] = scaled.astype(BF16)

    def weight(first, last):
        return w_ref[:, first * width:last * width]

    for m in (2, 3):
        restore(m)

    total = mask_ref.shape[1]
    at_row = lax.broadcasted_iota(jnp.int32, (rows, total), 0)
    at_lane = lax.broadcasted_iota(jnp.int32, (rows, total), 1)
    picks = jnp.where(at_lane == my_row * side + (at_row >> shift), 1.0, 0.0) + jnp.where(
        at_lane == my_col * side + (at_row & (side - 1)), 1.0, 0.0)
    kept = jnp.broadcast_to(mask_ref[...].astype(F32), (width, total)).astype(BF16)
    pair_mask = jnp.where(dot_t(picks.astype(BF16), kept) > 1.5, 1.0, 0.0)

    x = pair_ref[...].astype(F32)
    centered = x - jnp.mean(x, axis=-1, keepdims=True)
    pair_inverse = lax.rsqrt(jnp.mean(centered * centered, axis=-1, keepdims=True) + 1e-05)
    normed = centered * pair_inverse
    pair_normed = normed.astype(BF16)

    projected = dot(pair_normed, weight(2, 4))
    gate_r, value_r = projected[:, :width], projected[:, width:]
    sig_r = jax.nn.sigmoid(gate_r)
    masked_r = pair_mask * sig_r
    right = (masked_r * value_r).astype(BF16)
    own[...] = right

    @pl.when(elsewhere)
    def _():
        pl.semaphore_wait(barrier, 3 * (n - 1) + 1)

    @pl.when(diagonal)
    def _():
        pl.semaphore_wait(barrier, 3 * (n - 1))

    def send_right(d):
        return remote(0, own, rbuf.at[my_col], d, my_col, {"row": partner(my_row, d, n), "col": my_row})

    for d in reversed(range(1, n)):
        send_right(d).start()

    @pl.when(elsewhere)
    def _():
        send_right(0).start()

    @pl.when(diagonal)
    def _():
        rbuf[my_col] = right

    coef[2] = masked_r * value_r * (1.0 - sig_r)
    coef[3] = masked_r

    a = lax.broadcasted_iota(jnp.int32, (rows, rows), 0)
    b = lax.broadcasted_iota(jnp.int32, (rows, rows), 1)
    perm_ref[...] = jnp.where(b == ((a & (side - 1)) << shift) + (a >> shift), 1.0, 0.0).astype(BF16)
    loads[4].wait()
    for m in (0, 1):
        restore(m)
    projected = dot(pair_normed, weight(0, 2))
    gate_l, value_l = projected[:, :width], projected[:, width:]
    sig_l = jax.nn.sigmoid(gate_l)
    masked_l = pair_mask * sig_l
    left = (masked_l * value_l).astype(BF16)
    lbuf[my_col] = left

    def send_left(d):
        return remote(4, lbuf.at[my_col], lbuf.at[my_col], d, my_col, {"col": partner(my_col, d, n)})

    for d in reversed(range(1, n)):
        send_left(d).start()
    left_f[...] = left.astype(F32)
    coef[0] = masked_l * value_l * (1.0 - sig_l)
    coef[1] = masked_l

    for load in loads[5:]:
        load.wait()
    for m in (4, 5):
        restore(m)
    swapped = dot(perm_ref[...], pair_normed).astype(BF16)
    gate = jax.nn.sigmoid(dot(swapped, weight(4, 5)))
    upstream = dot(perm_ref[...], cot_ref[...])
    gated = upstream * gate
    keep[0] = gated * (1.0 - gate)
    grad_normed = dot_t(gated.astype(BF16), weight(5, 6))
    keep[1] = grad_normed - jnp.mean(grad_normed, axis=-1, keepdims=True)

    for d in range(n):
        c = partner(my_col, d, n)
        base = pl.multiple_of(c * rows, rows)
        if d > 0:
            wait_arrival(4, lbuf, c, "col")
        left_t[...] = dot(perm_ref[...], lbuf[c])
        if d > 0:
            wait_arrival(0, rbuf, c, "col")
        else:

            @pl.when(elsewhere)
            def _():
                wait_arrival(0, rbuf, my_col, "row")

        rf[pl.ds(base, rows), :] = rbuf[c].astype(F32)

        def emit(o, value, d=d):
            spot = (pl.ds(o, side), slice(None))
            upd[spot] = value if d == 0 else upd[spot] + value

        contract(side, rf, base, side, 1, left_t, 0, emit)

    update = upd[...]
    centered = update - jnp.mean(update, axis=-1, keepdims=True)
    inverse = lax.rsqrt(jnp.mean(centered * centered, axis=-1, keepdims=True) + 1e-05)
    update_normed = centered * inverse
    grad_normed = keep[1]
    second = jnp.mean(grad_normed * update_normed, axis=-1, keepdims=True)
    update_grad = (inverse * (grad_normed - update_normed * second)).astype(BF16)
    cbuf[my_col] = update_grad

    def send_update(d):
        return remote(2, cbuf.at[my_col], cbuf.at[my_col], d, my_col, {"col": partner(my_col, d, n)})

    for d in range(1, n):
        send_update(d).start()

    def send_grad(d):
        return remote(3, ebuf.at[d], gbuf.at[my_row], d, my_row, {"row": partner(my_col, d, n)})

    def send_left_grad(d):
        return remote(1, pbuf.at[d], hbuf.at[my_col], d, my_col, {"col": partner(my_col, d, n)})

    def right_part(d):
        c = partner(my_col, d, n)
        base = pl.multiple_of(c * rows, rows)
        if d > 0:
            wait_arrival(2, cbuf, c, "col")
        ugf[pl.ds(base, rows), :] = cbuf[c].astype(F32)

        def emit(o, value):
            ebuf[d, pl.ds(o, side), :] = value.astype(BF16)

        contract(side, ugf, base, side, 1, left_f, 0, emit)

        @pl.when(c != my_row)
        def _():
            send_grad(d).start()

        @pl.when(c == my_row)
        def _():
            gbuf[my_row] = ebuf[d]

    own_base = pl.multiple_of(my_col * rows, rows)

    def left_part(d):
        c = partner(my_col, d, n)

        def emit(o, value):
            if d == 0:
                lg_ref[pl.ds(o, side), :] = value
            else:
                pbuf[d, pl.ds(o, side), :] = value.astype(BF16)

        contract(side, ugf, own_base, 1, side, rf, pl.multiple_of(c * rows, rows), emit)
        if d > 0:
            send_left_grad(d).start()

    right_part(0)
    for d in reversed(range(1, n)):
        left_part(d)
    right_part(1)
    left_part(0)
    for d in range(2, n):
        right_part(d)

    grad_gate = keep[0] * dot(update_normed.astype(BF16), weight(5, 6))
    grad_gate = dot(perm_ref[...], grad_gate.astype(BF16)).astype(BF16)
    left_grad = lg_ref[...]
    for d in range(1, n):
        c = partner(my_col, d, n)
        wait_arrival(1, hbuf, c, "col")
        left_grad = left_grad + hbuf[c].astype(F32)
    normed_grad = (
        dot_t((left_grad * coef[0]).astype(BF16), weight(0, 1))
        + dot_t((left_grad * coef[1]).astype(BF16), weight(1, 2))
        + dot_t(grad_gate, weight(4, 5))
    )

    for d in range(1, n):
        wait_arrival(3, gbuf, partner(my_row, d, n), "row")
    right_grad = gbuf[0].astype(F32)
    for s in range(1, n):
        right_grad = right_grad + gbuf[s].astype(F32)
    normed_grad = (
        normed_grad
        + dot_t((right_grad * coef[2]).astype(BF16), weight(2, 3))
        + dot_t((right_grad * coef[3]).astype(BF16), weight(3, 4))
    )
    first = jnp.mean(normed_grad, axis=-1, keepdims=True)
    second = jnp.mean(normed_grad * normed, axis=-1, keepdims=True)
    out_ref[...] = pair_inverse * (normed_grad - first - normed * second)

    for d in range(1, n):
        send_right(d).wait_send()
        send_left(d).wait_send()
        send_update(d).wait_send()
        send_left_grad(d).wait_send()

    @pl.when(elsewhere)
    def _():
        send_right(0).wait_send()

    for d in range(n):

        @pl.when(partner(my_col, d, n) != my_row)
        def _():
            send_grad(d).wait_send()


def per_device(n, pair, cotangent, weight_codes, exponents, residue_mask):
    side = pair.shape[0]
    width = pair.shape[2]
    rows = side * side
    matrices = weight_codes.shape[0]
    slots = (n, rows, width)
    vmem = pl.BlockSpec(memory_space=pltpu.VMEM)
    out = pl.pallas_call(
        functools.partial(kernel, side, n),
        out_shape=jax.ShapeDtypeStruct((rows, width), F32),
        in_specs=[pl.BlockSpec(memory_space=pltpu.HBM)] * 5,
        out_specs=vmem,
        scratch_shapes=[
            pltpu.VMEM((rows, width), pair.dtype),
            pltpu.VMEM((rows, width), cotangent.dtype),
            pltpu.VMEM(weight_codes.shape, weight_codes.dtype),
            pltpu.VMEM(exponents.shape[::-1], exponents.dtype),
            pltpu.VMEM((1, residue_mask.shape[0]), residue_mask.dtype),
            pltpu.SemaphoreType.DMA((7,)),
            pltpu.VMEM((width, matrices * width), BF16),
            pltpu.VMEM((rows, rows), BF16),
            pltpu.VMEM((rows, width), BF16),
            pltpu.VMEM(slots, BF16),
            pltpu.VMEM((n * rows, width), F32),
            pltpu.VMEM(slots, BF16),
            pltpu.VMEM((rows, width), F32),
            pltpu.VMEM((rows, width), F32),
            pltpu.VMEM((rows, width), F32),
            pltpu.VMEM(slots, BF16),
            pltpu.VMEM((n * rows, width), F32),
            pltpu.VMEM(slots, BF16),
            pltpu.VMEM(slots, BF16),
            pltpu.VMEM(slots, BF16),
            pltpu.VMEM(slots, BF16),
            pltpu.VMEM((4, rows, width), F32),
            pltpu.VMEM((2, rows, width), F32),
            pltpu.VMEM((rows, width), F32),
            pltpu.SemaphoreType.DMA((5, n)),
            pltpu.SemaphoreType.DMA((5, n)),
        ],
        compiler_params=pltpu.CompilerParams(
            collective_id=0, has_side_effects=True, vmem_limit_bytes=VMEM_LIMIT
        ),
    )(
        pair.reshape(rows, width),
        cotangent.reshape(rows, width),
        weight_codes,
        exponents.T,
        residue_mask.reshape(1, -1),
    )
    return out.reshape(pair.shape)


def solution(mesh):
    in_specs = (P(("grp", "row"), "col", None), P(("grp", "row"), "col", None), P(), P(), P("grp"))
    out_specs = P(("grp", "row"), "col", None)
    n = mesh.shape["row"]
    assert n == mesh.shape["col"]
    return jax.shard_map(
        functools.partial(per_device, n), mesh=mesh, in_specs=in_specs, out_specs=out_specs, check_vma=False
    )
```

```python
import functools

import jax
import jax.numpy as jnp
from jax import lax
from jax.experimental import pallas as pl
from jax.experimental.pallas import tpu as pltpu
from jax.sharding import PartitionSpec as P

F32 = jnp.float32
BF16 = jnp.bfloat16
MESH = pl.DeviceIdType.MESH
GROUP = 8
VMEM_LIMIT = 63 * 1024 * 1024


def partner(me, d, n):
    if n & (n - 1):
        return lax.rem(me + d, n)
    out = me
    bit = 1
    while bit < n:
        if d & bit:
            out = out + bit - 2 * bit * lax.rem(lax.div(me, bit), 2)
        bit *= 2
    return out


def dot(a, b):
    return jnp.dot(a, b, preferred_element_type=F32)


def dot_t(a, b):
    return lax.dot_general(a, b, (((1,), (1,)), ((), ())), preferred_element_type=F32)


def contract(side, rows_ref, row_base, outer, inner, mat_ref, mat_base, emit):
    def body(g, carry):
        first = g * GROUP
        sums = [None] * GROUP
        start = row_base + first * outer
        for s in range(side):
            block = mat_ref[pl.ds(mat_base + s * side, side), :]
            for q in range(GROUP):
                row = rows_ref[pl.ds(start + q * outer + s * inner, 1), :]
                term = row * block
                sums[q] = term if sums[q] is None else sums[q] + term
        for q in range(GROUP):
            emit(pl.multiple_of((first + q) * side, side), sums[q])
        return carry

    lax.fori_loop(0, side // GROUP, body, 0)


def kernel(side, n, pair_hbm, cot_hbm, codes_hbm, exps_hbm, mask_hbm, out_ref,
           pair_ref, cot_ref, codes_ref, exps_ref, mask_ref, load_sem, w_ref, perm_ref,
           own, rbuf, rf, lbuf, left_f, left_t, upd, cbuf, ugf, ebuf, gbuf, pbuf, hbuf,
           coef, keep, lg_ref, send_sem, recv_sem):
    rows = side * side
    width = pair_ref.shape[1]
    matrices = codes_ref.shape[0]
    loads = [
        pltpu.make_async_copy(src, dst, load_sem.at[i])
        for i, (src, dst) in enumerate([
            (pair_hbm, pair_ref),
            (codes_hbm.at[pl.ds(2, 2)], codes_ref.at[pl.ds(2, 2)]),
            (exps_hbm, exps_ref),
            (mask_hbm, mask_ref),
            (codes_hbm.at[pl.ds(0, 2)], codes_ref.at[pl.ds(0, 2)]),
            (codes_hbm.at[pl.ds(4, matrices - 4)], codes_ref.at[pl.ds(4, matrices - 4)]),
            (cot_hbm, cot_ref),
        ])
    ]
    for load in loads:
        load.start()
    my_row = lax.axis_index("row")
    my_col = lax.axis_index("col")
    shift = side.bit_length() - 1

    diagonal = my_row == my_col
    elsewhere = jnp.logical_not(diagonal)
    barrier = pltpu.get_barrier_semaphore()

    def greet(target):
        pl.semaphore_signal(barrier, inc=1, device_id=target, device_id_type=MESH)

    for d in range(1, n):
        greet({"row": partner(my_row, d, n)})
        greet({"col": partner(my_col, d, n)})
        greet({"row": my_col, "col": partner(my_col, d, n)})

    @pl.when(elsewhere)
    def _():
        greet({"row": my_col, "col": my_col})

    def remote(stage, src, dst, send_slot, recv_slot, target):
        return pltpu.make_async_remote_copy(
            src_ref=src, dst_ref=dst,
            send_sem=send_sem.at[stage, send_slot], recv_sem=recv_sem.at[stage, recv_slot],
            device_id=target, device_id_type=MESH,
        )

    def wait_arrival(stage, buf, slot, axis):
        remote(stage, buf.at[slot], buf.at[slot], 0, slot, {axis: slot}).wait_recv()

    for load in loads[:4]:
        load.wait()

    factor = jnp.exp2(exps_ref[...].astype(F32))
    blocks = exps_ref.shape[0]
    depth = width // blocks

    def restore(m):
        for b in range(blocks):
            scaled = codes_ref[m, b * depth:(b + 1) * depth, :].astype(F32) * factor[b:b + 1, m:m + 1]
            w_ref[b * depth:(b + 1) * depth, m * width:(m + 1) * width] = scaled.astype(BF16)

    def weight(first, last):
        return w_ref[:, first * width:last * width]

    for m in (2, 3):
        restore(m)

    total = mask_ref.shape[1]
    at_row = lax.broadcasted_iota(jnp.int32, (rows, total), 0)
    at_lane = lax.broadcasted_iota(jnp.int32, (rows, total), 1)
    picks = jnp.where(at_lane == my_row * side + (at_row >> shift), 1.0, 0.0) + jnp.where(
        at_lane == my_col * side + (at_row & (side - 1)), 1.0, 0.0)
    kept = jnp.broadcast_to(mask_ref[...].astype(F32), (width, total)).astype(BF16)
    pair_mask = jnp.where(dot_t(picks.astype(BF16), kept) > 1.5, 1.0, 0.0)

    x = pair_ref[...].astype(F32)
    centered = x - jnp.mean(x, axis=-1, keepdims=True)
    pair_inverse = lax.rsqrt(jnp.mean(centered * centered, axis=-1, keepdims=True) + 1e-05)
    normed = centered * pair_inverse
    pair_normed = normed.astype(BF16)

    projected = dot(pair_normed, weight(2, 4))
    gate_r, value_r = projected[:, :width], projected[:, width:]
    sig_r = jax.nn.sigmoid(gate_r)
    masked_r = pair_mask * sig_r
    right = (masked_r * value_r).astype(BF16)
    own[...] = right

    @pl.when(elsewhere)
    def _():
        pl.semaphore_wait(barrier, 3 * (n - 1) + 1)

    @pl.when(diagonal)
    def _():
        pl.semaphore_wait(barrier, 3 * (n - 1))

    def send_right(d):
        return remote(0, own, rbuf.at[my_col], d, my_col, {"row": partner(my_row, d, n), "col": my_row})

    for d in reversed(range(1, n)):
        send_right(d).start()

    @pl.when(elsewhere)
    def _():
        send_right(0).start()

    @pl.when(diagonal)
    def _():
        rbuf[my_col] = right

    coef[2] = masked_r * value_r * (1.0 - sig_r)
    coef[3] = masked_r

    a = lax.broadcasted_iota(jnp.int32, (rows, rows), 0)
    b = lax.broadcasted_iota(jnp.int32, (rows, rows), 1)
    perm_ref[...] = jnp.where(b == ((a & (side - 1)) << shift) + (a >> shift), 1.0, 0.0).astype(BF16)
    loads[4].wait()
    for m in (0, 1):
        restore(m)
    projected = dot(pair_normed, weight(0, 2))
    gate_l, value_l = projected[:, :width], projected[:, width:]
    sig_l = jax.nn.sigmoid(gate_l)
    masked_l = pair_mask * sig_l
    left = (masked_l * value_l).astype(BF16)
    lbuf[my_col] = left

    direct = [1] + list(range(2, n, 2))
    sibling = {"col": partner(my_col, 1, n)}

    def send_left(d):
        if d in direct:
            return remote(4, lbuf.at[my_col], lbuf.at[my_col], d, my_col, {"col": partner(my_col, d, n)})
        c = partner(my_col, d - 1, n)
        return remote(4, lbuf.at[c], lbuf.at[c], d, c, sibling)

    for d in direct:
        send_left(d).start()
    left_f[...] = left.astype(F32)
    coef[0] = masked_l * value_l * (1.0 - sig_l)
    coef[1] = masked_l

    for load in loads[5:]:
        load.wait()
    for m in (4, 5):
        restore(m)
    swapped = dot(perm_ref[...], pair_normed).astype(BF16)
    gate = jax.nn.sigmoid(dot(swapped, weight(4, 5)))
    upstream = dot(perm_ref[...], cot_ref[...])
    gated = upstream * gate
    keep[0] = gated * (1.0 - gate)
    grad_normed = dot_t(gated.astype(BF16), weight(5, 6))
    keep[1] = grad_normed - jnp.mean(grad_normed, axis=-1, keepdims=True)

    for d in range(2, n, 2):
        wait_arrival(4, lbuf, partner(my_col, d, n), "col")
        send_left(d + 1).start()

    for d in range(n):
        c = partner(my_col, d, n)
        base = pl.multiple_of(c * rows, rows)
        if d % 2:
            wait_arrival(4, lbuf, c, "col")
        left_t[...] = dot(perm_ref[...], lbuf[c])
        if d > 0:
            wait_arrival(0, rbuf, c, "col")
        else:

            @pl.when(elsewhere)
            def _():
                wait_arrival(0, rbuf, my_col, "row")

        rf[pl.ds(base, rows), :] = rbuf[c].astype(F32)

        def emit(o, value, d=d):
            spot = (pl.ds(o, side), slice(None))
            upd[spot] = value if d == 0 else upd[spot] + value

        contract(side, rf, base, side, 1, left_t, 0, emit)

    update = upd[...]
    centered = update - jnp.mean(update, axis=-1, keepdims=True)
    inverse = lax.rsqrt(jnp.mean(centered * centered, axis=-1, keepdims=True) + 1e-05)
    update_normed = centered * inverse
    grad_normed = keep[1]
    second = jnp.mean(grad_normed * update_normed, axis=-1, keepdims=True)
    update_grad = (inverse * (grad_normed - update_normed * second)).astype(BF16)
    cbuf[my_col] = update_grad

    def send_update(d):
        if d in direct:
            return remote(2, cbuf.at[my_col], cbuf.at[my_col], d, my_col, {"col": partner(my_col, d, n)})
        c = partner(my_col, d - 1, n)
        return remote(2, cbuf.at[c], cbuf.at[c], d, c, sibling)

    for d in direct:
        send_update(d).start()

    def send_grad(d):
        return remote(3, ebuf.at[d], gbuf.at[my_row], d, my_row, {"row": partner(my_col, d, n)})

    def send_left_grad(d):
        return remote(1, pbuf.at[d], hbuf.at[my_col], d, my_col, {"col": partner(my_col, d, n)})

    def right_part(d):
        c = partner(my_col, d, n)
        base = pl.multiple_of(c * rows, rows)
        if d % 2:
            wait_arrival(2, cbuf, c, "col")
        ugf[pl.ds(base, rows), :] = cbuf[c].astype(F32)

        def emit(o, value):
            ebuf[d, pl.ds(o, side), :] = value.astype(BF16)

        contract(side, ugf, base, side, 1, left_f, 0, emit)

        @pl.when(c != my_row)
        def _():
            send_grad(d).start()

        @pl.when(c == my_row)
        def _():
            gbuf[my_row] = ebuf[d]

    own_base = pl.multiple_of(my_col * rows, rows)

    def left_part(d):
        c = partner(my_col, d, n)

        def emit(o, value):
            if d == 0:
                lg_ref[pl.ds(o, side), :] = value
            else:
                pbuf[d, pl.ds(o, side), :] = value.astype(BF16)

        contract(side, ugf, own_base, 1, side, rf, pl.multiple_of(c * rows, rows), emit)
        if d > 0:
            send_left_grad(d).start()

    right_part(0)
    for d in reversed(range(1, n)):
        left_part(d)
    right_part(1)
    for d in range(2, n, 2):
        wait_arrival(2, cbuf, partner(my_col, d, n), "col")
        send_update(d + 1).start()
    right_part(2)
    left_part(0)
    for d in range(3, n):
        right_part(d)

    grad_gate = keep[0] * dot(update_normed.astype(BF16), weight(5, 6))
    grad_gate = dot(perm_ref[...], grad_gate.astype(BF16)).astype(BF16)
    left_grad = lg_ref[...]
    for d in range(1, n):
        c = partner(my_col, d, n)
        wait_arrival(1, hbuf, c, "col")
        left_grad = left_grad + hbuf[c].astype(F32)
    normed_grad = (
        dot_t((left_grad * coef[0]).astype(BF16), weight(0, 1))
        + dot_t((left_grad * coef[1]).astype(BF16), weight(1, 2))
        + dot_t(grad_gate, weight(4, 5))
    )

    for d in range(1, n):
        wait_arrival(3, gbuf, partner(my_row, d, n), "row")
    right_grad = gbuf[0].astype(F32)
    for s in range(1, n):
        right_grad = right_grad + gbuf[s].astype(F32)
    normed_grad = (
        normed_grad
        + dot_t((right_grad * coef[2]).astype(BF16), weight(2, 3))
        + dot_t((right_grad * coef[3]).astype(BF16), weight(3, 4))
    )
    first = jnp.mean(normed_grad, axis=-1, keepdims=True)
    second = jnp.mean(normed_grad * normed, axis=-1, keepdims=True)
    out_ref[...] = pair_inverse * (normed_grad - first - normed * second)

    for d in range(1, n):
        send_right(d).wait_send()
        send_left(d).wait_send()
        send_update(d).wait_send()
        send_left_grad(d).wait_send()

    @pl.when(elsewhere)
    def _():
        send_right(0).wait_send()

    for d in range(n):

        @pl.when(partner(my_col, d, n) != my_row)
        def _():
            send_grad(d).wait_send()


def per_device(n, pair, cotangent, weight_codes, exponents, residue_mask):
    side = pair.shape[0]
    width = pair.shape[2]
    rows = side * side
    matrices = weight_codes.shape[0]
    slots = (n, rows, width)
    vmem = pl.BlockSpec(memory_space=pltpu.VMEM)
    out = pl.pallas_call(
        functools.partial(kernel, side, n),
        out_shape=jax.ShapeDtypeStruct((rows, width), F32),
        in_specs=[pl.BlockSpec(memory_space=pltpu.HBM)] * 5,
        out_specs=vmem,
        scratch_shapes=[
            pltpu.VMEM((rows, width), pair.dtype),
            pltpu.VMEM((rows, width), cotangent.dtype),
            pltpu.VMEM(weight_codes.shape, weight_codes.dtype),
            pltpu.VMEM(exponents.shape[::-1], exponents.dtype),
            pltpu.VMEM((1, residue_mask.shape[0]), residue_mask.dtype),
            pltpu.SemaphoreType.DMA((7,)),
            pltpu.VMEM((width, matrices * width), BF16),
            pltpu.VMEM((rows, rows), BF16),
            pltpu.VMEM((rows, width), BF16),
            pltpu.VMEM(slots, BF16),
            pltpu.VMEM((n * rows, width), F32),
            pltpu.VMEM(slots, BF16),
            pltpu.VMEM((rows, width), F32),
            pltpu.VMEM((rows, width), F32),
            pltpu.VMEM((rows, width), F32),
            pltpu.VMEM(slots, BF16),
            pltpu.VMEM((n * rows, width), F32),
            pltpu.VMEM(slots, BF16),
            pltpu.VMEM(slots, BF16),
            pltpu.VMEM(slots, BF16),
            pltpu.VMEM(slots, BF16),
            pltpu.VMEM((4, rows, width), F32),
            pltpu.VMEM((2, rows, width), F32),
            pltpu.VMEM((rows, width), F32),
            pltpu.SemaphoreType.DMA((5, n)),
            pltpu.SemaphoreType.DMA((5, n)),
        ],
        compiler_params=pltpu.CompilerParams(
            collective_id=0, has_side_effects=True, vmem_limit_bytes=VMEM_LIMIT
        ),
    )(
        pair.reshape(rows, width),
        cotangent.reshape(rows, width),
        weight_codes,
        exponents.T,
        residue_mask.reshape(1, -1),
    )
    return out.reshape(pair.shape)


def solution(mesh):
    in_specs = (P(("grp", "row"), "col", None), P(("grp", "row"), "col", None), P(), P(), P("grp"))
    out_specs = P(("grp", "row"), "col", None)
    n = mesh.shape["row"]
    assert n == mesh.shape["col"] and n & (n - 1) == 0
    return jax.shard_map(
        functools.partial(per_device, n), mesh=mesh, in_specs=in_specs, out_specs=out_specs, check_vma=False
    )
```

```python
import functools

import jax
import jax.numpy as jnp
from jax import lax
from jax.experimental import pallas as pl
from jax.experimental.pallas import tpu as pltpu
from jax.sharding import PartitionSpec as P

F32 = jnp.float32
BF16 = jnp.bfloat16
MESH = pl.DeviceIdType.MESH
GROUP = 8
VMEM_LIMIT = 63 * 1024 * 1024


def partner(me, d, n):
    if n & (n - 1):
        return lax.rem(me + d, n)
    out = me
    bit = 1
    while bit < n:
        if d & bit:
            out = out + bit - 2 * bit * lax.rem(lax.div(me, bit), 2)
        bit *= 2
    return out


def dot(a, b):
    return jnp.dot(a, b, preferred_element_type=F32)


def dot_t(a, b):
    return lax.dot_general(a, b, (((1,), (1,)), ((), ())), preferred_element_type=F32)


def contract(side, rows_ref, row_base, outer, inner, mat_ref, mat_base, emit):
    def body(g, carry):
        first = g * GROUP
        sums = [None] * GROUP
        start = row_base + first * outer
        for s in range(side):
            block = mat_ref[pl.ds(mat_base + s * side, side), :]
            for q in range(GROUP):
                row = rows_ref[pl.ds(start + q * outer + s * inner, 1), :]
                term = row * block
                sums[q] = term if sums[q] is None else sums[q] + term
        for q in range(GROUP):
            emit(pl.multiple_of((first + q) * side, side), sums[q])
        return carry

    lax.fori_loop(0, side // GROUP, body, 0)


def kernel(side, n, pair_hbm, cot_hbm, codes_hbm, exps_hbm, mask_hbm, out_ref,
           pair_ref, cot_ref, codes_ref, exps_ref, mask_ref, load_sem, w_ref, perm_ref,
           own, rbuf, rf, lbuf, left_f, left_t, upd, cbuf, ugf, ebuf, gbuf, pbuf, hbuf,
           coef, keep, lg_ref, send_sem, recv_sem):
    rows = side * side
    width = pair_ref.shape[1]
    matrices = codes_ref.shape[0]
    loads = [
        pltpu.make_async_copy(src, dst, load_sem.at[i])
        for i, (src, dst) in enumerate([
            (pair_hbm, pair_ref),
            (codes_hbm.at[pl.ds(2, 2)], codes_ref.at[pl.ds(2, 2)]),
            (exps_hbm, exps_ref),
            (mask_hbm, mask_ref),
            (codes_hbm.at[pl.ds(0, 2)], codes_ref.at[pl.ds(0, 2)]),
            (codes_hbm.at[pl.ds(4, matrices - 4)], codes_ref.at[pl.ds(4, matrices - 4)]),
            (cot_hbm, cot_ref),
        ])
    ]
    for load in loads:
        load.start()
    my_row = lax.axis_index("row")
    my_col = lax.axis_index("col")
    shift = side.bit_length() - 1

    diagonal = my_row == my_col
    elsewhere = jnp.logical_not(diagonal)
    barrier = pltpu.get_barrier_semaphore()

    def greet(target):
        pl.semaphore_signal(barrier, inc=1, device_id=target, device_id_type=MESH)

    for d in range(1, n):
        greet({"row": partner(my_row, d, n)})
        greet({"col": partner(my_col, d, n)})
        greet({"row": my_col, "col": partner(my_col, d, n)})

    @pl.when(elsewhere)
    def _():
        greet({"row": my_col, "col": my_col})

    def remote(stage, src, dst, send_slot, recv_slot, target):
        return pltpu.make_async_remote_copy(
            src_ref=src, dst_ref=dst,
            send_sem=send_sem.at[stage, send_slot], recv_sem=recv_sem.at[stage, recv_slot],
            device_id=target, device_id_type=MESH,
        )

    def wait_arrival(stage, buf, slot, axis):
        remote(stage, buf.at[slot], buf.at[slot], 0, slot, {axis: slot}).wait_recv()

    for load in loads[:4]:
        load.wait()

    factor = jnp.exp2(exps_ref[...].astype(F32))
    blocks = exps_ref.shape[0]
    depth = width // blocks

    def restore(m):
        for b in range(blocks):
            scaled = codes_ref[m, b * depth:(b + 1) * depth, :].astype(F32) * factor[b:b + 1, m:m + 1]
            w_ref[b * depth:(b + 1) * depth, m * width:(m + 1) * width] = scaled.astype(BF16)

    def weight(first, last):
        return w_ref[:, first * width:last * width]

    for m in (2, 3):
        restore(m)

    total = mask_ref.shape[1]
    at_row = lax.broadcasted_iota(jnp.int32, (rows, total), 0)
    at_lane = lax.broadcasted_iota(jnp.int32, (rows, total), 1)
    picks = jnp.where(at_lane == my_row * side + (at_row >> shift), 1.0, 0.0) + jnp.where(
        at_lane == my_col * side + (at_row & (side - 1)), 1.0, 0.0)
    kept = jnp.broadcast_to(mask_ref[...].astype(F32), (width, total)).astype(BF16)
    pair_mask = jnp.where(dot_t(picks.astype(BF16), kept) > 1.5, 1.0, 0.0)

    x = pair_ref[...].astype(F32)
    centered = x - jnp.mean(x, axis=-1, keepdims=True)
    pair_inverse = lax.rsqrt(jnp.mean(centered * centered, axis=-1, keepdims=True) + 1e-05)
    normed = centered * pair_inverse
    pair_normed = normed.astype(BF16)

    projected = dot(pair_normed, weight(2, 4))
    gate_r, value_r = projected[:, :width], projected[:, width:]
    sig_r = jax.nn.sigmoid(gate_r)
    masked_r = pair_mask * sig_r
    right = (masked_r * value_r).astype(BF16)
    own[...] = right

    @pl.when(elsewhere)
    def _():
        pl.semaphore_wait(barrier, 3 * (n - 1) + 1)

    @pl.when(diagonal)
    def _():
        pl.semaphore_wait(barrier, 3 * (n - 1))

    def send_right(d):
        return remote(0, own, rbuf.at[my_col], d, my_col, {"row": partner(my_row, d, n), "col": my_row})

    for d in reversed(range(1, n)):
        send_right(d).start()

    @pl.when(elsewhere)
    def _():
        send_right(0).start()

    @pl.when(diagonal)
    def _():
        rbuf[my_col] = right

    coef[2] = masked_r * value_r * (1.0 - sig_r)
    coef[3] = masked_r

    a = lax.broadcasted_iota(jnp.int32, (rows, rows), 0)
    b = lax.broadcasted_iota(jnp.int32, (rows, rows), 1)
    perm_ref[...] = jnp.where(b == ((a & (side - 1)) << shift) + (a >> shift), 1.0, 0.0).astype(BF16)
    loads[4].wait()
    for m in (0, 1):
        restore(m)
    projected = dot(pair_normed, weight(0, 2))
    gate_l, value_l = projected[:, :width], projected[:, width:]
    sig_l = jax.nn.sigmoid(gate_l)
    masked_l = pair_mask * sig_l
    left = (masked_l * value_l).astype(BF16)
    lbuf[my_col] = left

    direct = [1] + list(range(2, n, 2))
    sibling = {"col": partner(my_col, 1, n)}

    def send_left(d):
        if d in direct:
            return remote(4, lbuf.at[my_col], lbuf.at[my_col], d, my_col, {"col": partner(my_col, d, n)})
        c = partner(my_col, d - 1, n)
        return remote(4, lbuf.at[c], lbuf.at[c], d, c, sibling)

    for d in direct:
        send_left(d).start()
    left_f[...] = left.astype(F32)
    coef[0] = masked_l * value_l * (1.0 - sig_l)
    coef[1] = masked_l

    for load in loads[5:]:
        load.wait()
    for m in (4, 5):
        restore(m)
    swapped = dot(perm_ref[...], pair_normed).astype(BF16)
    gate = jax.nn.sigmoid(dot(swapped, weight(4, 5)))
    upstream = dot(perm_ref[...], cot_ref[...])
    gated = upstream * gate
    keep[0] = gated * (1.0 - gate)
    grad_normed = dot_t(gated.astype(BF16), weight(5, 6))
    keep[1] = grad_normed - jnp.mean(grad_normed, axis=-1, keepdims=True)

    for d in range(2, n, 2):
        wait_arrival(4, lbuf, partner(my_col, d, n), "col")
        send_left(d + 1).start()

    for d in range(n):
        c = partner(my_col, d, n)
        base = pl.multiple_of(c * rows, rows)
        if d % 2:
            wait_arrival(4, lbuf, c, "col")
        left_t[...] = dot(perm_ref[...], lbuf[c])
        if d > 0:
            wait_arrival(0, rbuf, c, "col")
        else:

            @pl.when(elsewhere)
            def _():
                wait_arrival(0, rbuf, my_col, "row")

        rf[pl.ds(base, rows), :] = rbuf[c].astype(F32)

        def emit(o, value, d=d):
            spot = (pl.ds(o, side), slice(None))
            upd[spot] = value if d == 0 else upd[spot] + value

        contract(side, rf, base, side, 1, left_t, 0, emit)

    update = upd[...]
    centered = update - jnp.mean(update, axis=-1, keepdims=True)
    inverse = lax.rsqrt(jnp.mean(centered * centered, axis=-1, keepdims=True) + 1e-05)
    update_normed = centered * inverse
    grad_normed = keep[1]
    second = jnp.mean(grad_normed * update_normed, axis=-1, keepdims=True)
    update_grad = (inverse * (grad_normed - update_normed * second)).astype(BF16)
    cbuf[my_col] = update_grad

    def send_update(d):
        if d in direct:
            return remote(2, cbuf.at[my_col], cbuf.at[my_col], d, my_col, {"col": partner(my_col, d, n)})
        c = partner(my_col, d - 1, n)
        return remote(2, cbuf.at[c], cbuf.at[c], d, c, sibling)

    for d in direct:
        send_update(d).start()

    def send_grad(d):
        return remote(3, ebuf.at[d], gbuf.at[my_row], d, my_row, {"row": partner(my_col, d, n)})

    def send_left_grad(d):
        return remote(1, pbuf.at[d], hbuf.at[my_col], d, my_col, {"col": partner(my_col, d, n)})

    def right_part(d):
        c = partner(my_col, d, n)
        base = pl.multiple_of(c * rows, rows)
        if d % 2:
            wait_arrival(2, cbuf, c, "col")
        ugf[pl.ds(base, rows), :] = cbuf[c].astype(F32)

        def emit(o, value):
            ebuf[d, pl.ds(o, side), :] = value.astype(BF16)

        contract(side, ugf, base, side, 1, left_f, 0, emit)

        @pl.when(c != my_row)
        def _():
            send_grad(d).start()

        @pl.when(c == my_row)
        def _():
            gbuf[my_row] = ebuf[d]

    own_base = pl.multiple_of(my_col * rows, rows)

    def left_part(d):
        c = partner(my_col, d, n)

        def emit(o, value):
            if d == 0:
                lg_ref[pl.ds(o, side), :] = value
            else:
                pbuf[d, pl.ds(o, side), :] = value.astype(BF16)

        contract(side, ugf, own_base, 1, side, rf, pl.multiple_of(c * rows, rows), emit)
        if d > 0:
            send_left_grad(d).start()

    right_part(0)
    for d in reversed(range(2, n)):
        left_part(d)
    right_part(1)
    for d in range(2, n, 2):
        wait_arrival(2, cbuf, partner(my_col, d, n), "col")
        send_update(d + 1).start()
    for d in range(2, n):
        right_part(d)
    left_part(1)
    left_part(0)

    grad_gate = keep[0] * dot(update_normed.astype(BF16), weight(5, 6))
    grad_gate = dot(perm_ref[...], grad_gate.astype(BF16)).astype(BF16)
    left_grad = lg_ref[...]
    for d in range(1, n):
        c = partner(my_col, d, n)
        wait_arrival(1, hbuf, c, "col")
        left_grad = left_grad + hbuf[c].astype(F32)
    normed_grad = (
        dot_t((left_grad * coef[0]).astype(BF16), weight(0, 1))
        + dot_t((left_grad * coef[1]).astype(BF16), weight(1, 2))
        + dot_t(grad_gate, weight(4, 5))
    )

    for d in range(1, n):
        wait_arrival(3, gbuf, partner(my_row, d, n), "row")
    right_grad = gbuf[0].astype(F32)
    for s in range(1, n):
        right_grad = right_grad + gbuf[s].astype(F32)
    normed_grad = (
        normed_grad
        + dot_t((right_grad * coef[2]).astype(BF16), weight(2, 3))
        + dot_t((right_grad * coef[3]).astype(BF16), weight(3, 4))
    )
    first = jnp.mean(normed_grad, axis=-1, keepdims=True)
    second = jnp.mean(normed_grad * normed, axis=-1, keepdims=True)
    out_ref[...] = pair_inverse * (normed_grad - first - normed * second)

    for d in range(1, n):
        send_right(d).wait_send()
        send_left(d).wait_send()
        send_update(d).wait_send()
        send_left_grad(d).wait_send()

    @pl.when(elsewhere)
    def _():
        send_right(0).wait_send()

    for d in range(n):

        @pl.when(partner(my_col, d, n) != my_row)
        def _():
            send_grad(d).wait_send()


def per_device(n, pair, cotangent, weight_codes, exponents, residue_mask):
    side = pair.shape[0]
    width = pair.shape[2]
    rows = side * side
    matrices = weight_codes.shape[0]
    slots = (n, rows, width)
    vmem = pl.BlockSpec(memory_space=pltpu.VMEM)
    out = pl.pallas_call(
        functools.partial(kernel, side, n),
        out_shape=jax.ShapeDtypeStruct((rows, width), F32),
        in_specs=[pl.BlockSpec(memory_space=pltpu.HBM)] * 5,
        out_specs=vmem,
        scratch_shapes=[
            pltpu.VMEM((rows, width), pair.dtype),
            pltpu.VMEM((rows, width), cotangent.dtype),
            pltpu.VMEM(weight_codes.shape, weight_codes.dtype),
            pltpu.VMEM(exponents.shape[::-1], exponents.dtype),
            pltpu.VMEM((1, residue_mask.shape[0]), residue_mask.dtype),
            pltpu.SemaphoreType.DMA((7,)),
            pltpu.VMEM((width, matrices * width), BF16),
            pltpu.VMEM((rows, rows), BF16),
            pltpu.VMEM((rows, width), BF16),
            pltpu.VMEM(slots, BF16),
            pltpu.VMEM((n * rows, width), F32),
            pltpu.VMEM(slots, BF16),
            pltpu.VMEM((rows, width), F32),
            pltpu.VMEM((rows, width), F32),
            pltpu.VMEM((rows, width), F32),
            pltpu.VMEM(slots, BF16),
            pltpu.VMEM((n * rows, width), F32),
            pltpu.VMEM(slots, BF16),
            pltpu.VMEM(slots, BF16),
            pltpu.VMEM(slots, BF16),
            pltpu.VMEM(slots, BF16),
            pltpu.VMEM((4, rows, width), F32),
            pltpu.VMEM((2, rows, width), F32),
            pltpu.VMEM((rows, width), F32),
            pltpu.SemaphoreType.DMA((5, n)),
            pltpu.SemaphoreType.DMA((5, n)),
        ],
        compiler_params=pltpu.CompilerParams(
            collective_id=0, has_side_effects=True, vmem_limit_bytes=VMEM_LIMIT
        ),
    )(
        pair.reshape(rows, width),
        cotangent.reshape(rows, width),
        weight_codes,
        exponents.T,
        residue_mask.reshape(1, -1),
    )
    return out.reshape(pair.shape)


def solution(mesh):
    in_specs = (P(("grp", "row"), "col", None), P(("grp", "row"), "col", None), P(), P(), P("grp"))
    out_specs = P(("grp", "row"), "col", None)
    n = mesh.shape["row"]
    assert n == mesh.shape["col"] and n & (n - 1) == 0
    return jax.shard_map(
        functools.partial(per_device, n), mesh=mesh, in_specs=in_specs, out_specs=out_specs, check_vma=False
    )
```
